32 devices in a mesh: seq: 8 (over z, x), batch: 4 (over y, core).
Axes of the slice: x: 2, y: 2, z: 4, core: 2. Of those that a mesh axis runs over, the one named last changes fastest.
Arguments:
- hidden: bfloat16 [4, 2048, 2048], P('batch', 'seq'), may hold values from -6 to 6
- in_weight: bfloat16 [1024, 4352], P('batch'), may hold values from -0.1875 to 0.1875
- dt_weight: bfloat16 [1024, 32], replicated, may hold values from -0.1875 to 0.1875
- conv_weight: float32 [4, 2304], replicated, may hold values from -3 to 3
- conv_bias: float32 [2304], replicated, may hold values from -3 to 3
- dt_bias: float32 [32], replicated, may hold values from -1 to 1
- a_log: float32 [32], replicated
- d_skip: float32 [32], replicated, may hold values from 0.5 to 1.5
- norm_gain: float32 [2048], replicated, may hold values from 0.1 to 1.9
- out_weight: bfloat16 [2048, 1024], P('batch'), may hold values from -0.125 to 0.125
Outputs:
- mixed: bfloat16 [4, 2048, 2048], P('batch', 'seq')
The draws below stay inside these ranges and needn't reach their ends.
All inputs are finite; a program needn't handle non-finite values.
Results may differ from the reference program's by a relative error of at most 0.0062.
Values may be sent and summed in bfloat16 or wider, within the bound.
A program may use at most 320 MiB of HBM per device.

```python
import math
import jax
import jax.numpy as jnp
from jax import lax

D = 1024
INNER = 2048
HEADS = 32
STATE = 128
SPAN = 128
HEADDIM = 64
CONVW = 2304
SEQLEN = 2048
BATCH = 4


def draw_a_log(key, part):
    pick_key, slow_key, fast_key = jax.random.split(key, 3)
    share = 0.5
    slow_rates = jax.random.uniform(slow_key, (HEADS,), jnp.float32, 0.1, 1.5) / SEQLEN
    fast_rates = jnp.exp(jax.random.uniform(fast_key, (HEADS,), jnp.float32, math.log(1.0 / 50.0), math.log(1.0 / 20.0)))
    slow_heads = jax.random.bernoulli(pick_key, share, (HEADS,))
    return jnp.log(jnp.where(slow_heads, slow_rates, fast_rates))


def level_of(stream_key, shape, cuts, smallest, high):
    gain = 1.0
    for dim, shards_of in cuts:
        draws = jax.random.uniform(jax.random.fold_in(jax.random.fold_in(stream_key, 6), dim), (shards_of,), jnp.float32, smallest / len(cuts), high / len(cuts))
        gain = gain * jnp.repeat(jnp.exp(draws), shape[dim] // shards_of).reshape((-1,) + (1,) * (len(shape) - 1 - dim))
    return gain


def noise(key, shape, width, limit, shards=(), kind=jnp.bfloat16):
    values = width * jax.random.normal(key, shape, jnp.float32)
    if shards:
        values = values * level_of(key, shape, shards, -0.22, 0.18)
    return jnp.clip(values, -limit, limit).astype(kind)


def setup_inputs(seed: int = 0) -> dict:
    seeds = jax.random.split(jax.random.key(seed), 11)
    hidden = noise(seeds[0], (BATCH, SEQLEN, 2 * D), 1.0, 6.0, ((0, 4), (1, 8)))
    in_weight = noise(seeds[1], (D, 2 * INNER + 2 * STATE), D ** -0.5, 0.1875, ((0, 4),))
    dt_weight = noise(seeds[2], (D, HEADS), D ** -0.5, 0.1875)
    conv_weight = noise(seeds[3], (4, CONVW), 4 ** -0.5, 3.0, (), jnp.float32)
    conv_bias = noise(seeds[4], (CONVW,), 0.5, 3.0, (), jnp.float32)
    dt_bias = jnp.clip(jax.random.uniform(seeds[5], (HEADS,), jnp.float32, -1.0, 1.0), -1.0, 1.0)
    a_log = draw_a_log(jax.random.fold_in(seeds[10], 71), 0)
    d_skip = jnp.clip(jax.random.uniform(seeds[7], (HEADS,), jnp.float32, 0.5, 1.5), 0.5, 1.5)
    norm_gain = jnp.clip(1.0 + 0.18 * jax.random.normal(seeds[8], (INNER,), jnp.float32), 0.1, 1.9)
    out_weight = noise(seeds[9], (INNER, D), INNER ** -0.5, 0.125, ((0, 4),))
    return dict(hidden=hidden, in_weight=in_weight, dt_weight=dt_weight, conv_weight=conv_weight, conv_bias=conv_bias, dt_bias=dt_bias, a_log=a_log, d_skip=d_skip, norm_gain=norm_gain, out_weight=out_weight)


def conv_act(conv_in, conv_weight, conv_bias, reverse):
    length = conv_in.shape[0]
    padded = jnp.pad(conv_in, ((3, 3), (0, 0)))
    running = conv_bias
    for tap_index in range(4):
        offset = 6 - tap_index if reverse else tap_index
        running = running + conv_weight[tap_index] * padded[offset:offset + length]
    return jax.nn.silu(running).astype(jnp.bfloat16)

def one_span(inputs):
    span_vals, write_vec, read_vec, step_rates, cumulate = inputs
    scores = jnp.dot(read_vec, write_vec.T, preferred_element_type=jnp.float32)
    causal = lax.broadcasted_iota(jnp.int32, (SPAN, SPAN), 0) >= lax.broadcasted_iota(jnp.int32, (SPAN, SPAN), 1)
    decay_mask = jnp.exp(jnp.where(causal[None], cumulate[:, :, None] - cumulate[:, None, :], -jnp.inf))
    mixing = lax.optimization_barrier((scores[None] * decay_mask * step_rates[:, None, :]).astype(jnp.bfloat16))
    inner_out = jnp.einsum('hqs,shp->qhp', mixing.astype(jnp.float32), span_vals.astype(jnp.float32))
    scaled = jnp.exp(cumulate[:, -1:] - cumulate) * step_rates
    weighted = lax.optimization_barrier((write_vec[None] * scaled[:, :, None]).astype(jnp.bfloat16))
    span_state = jnp.einsum('shp,hsn->hpn', span_vals.astype(jnp.float32), weighted.astype(jnp.float32))
    return (inner_out, span_state)

def advance(state_now, inputs):
    growth_step, fresh_state = inputs
    return (growth_step[:, None, None] * state_now + fresh_state, state_now)

def scan_core(act, step_dt, decay_rate, d_skip):
    length = act.shape[0]
    span_count = length // SPAN
    values = act[:, :INNER].reshape(span_count, SPAN, HEADS, HEADDIM)
    write_vec = act[:, INNER:INNER + STATE].reshape(span_count, SPAN, STATE)
    read_vec = act[:, INNER + STATE:].reshape(span_count, SPAN, STATE)
    step_rates = step_dt.reshape(HEADS, span_count, SPAN).transpose(1, 0, 2)
    cumulate = jnp.cumsum(step_rates * decay_rate[None, :, None], axis=2)
    inner_out, states = lax.map(one_span, (values, write_vec, read_vec, step_rates, cumulate))
    growth = jnp.exp(cumulate[:, :, -1])
    start_state = jnp.zeros((HEADS, HEADDIM, STATE), jnp.float32)
    _, entries = lax.scan(advance, start_state, (growth, states))
    rounded = lax.optimization_barrier(entries.astype(jnp.bfloat16))
    from_state = jnp.einsum('kqn,khpn->kqhp', read_vec.astype(jnp.float32), rounded.astype(jnp.float32))
    from_state = from_state * jnp.exp(cumulate).transpose(0, 2, 1)[..., None]
    result = inner_out + from_state + d_skip[None, None, :, None] * values.astype(jnp.float32)
    return result.reshape(length, INNER)

def gate_norm(result, gate_part, norm_gain):
    gated = result * jax.nn.silu(gate_part.astype(jnp.float32))
    return gated * lax.rsqrt(lax.optimization_barrier(jnp.mean(gated * gated, axis=-1, keepdims=True)) + 1e-05) * norm_gain

def reference(hidden, in_weight, dt_weight, conv_weight, conv_bias, dt_bias, a_log, d_skip, norm_gain, out_weight):
    forward_half = hidden[:, :, :D]
    reverse_half = jnp.flip(hidden[:, :, D:], -1)
    streams = jnp.concatenate([forward_half, reverse_half], 0)
    decay_rate = -jnp.exp(a_log)

    def mixer_pass(stream_rows):
        projected = jnp.dot(stream_rows, in_weight, preferred_element_type=jnp.float32).astype(jnp.bfloat16)
        gate_part = projected[:, :INNER]
        conv_in = projected[:, INNER:]
        step_dt = jax.nn.softplus(jnp.dot(stream_rows, dt_weight, preferred_element_type=jnp.float32) + dt_bias).T
        ahead_act = conv_act(conv_in, conv_weight, conv_bias, False)
        behind_act = conv_act(conv_in, conv_weight, conv_bias, True)
        forward_y = scan_core(ahead_act, step_dt, decay_rate, d_skip)
        backward_y = jnp.flip(scan_core(jnp.flip(behind_act, 0), jnp.flip(step_dt, 1), decay_rate, d_skip), 0)
        combined = (gate_norm(forward_y, gate_part, norm_gain) + gate_norm(backward_y, gate_part, norm_gain)).astype(jnp.bfloat16)
        return jnp.dot(combined, out_weight, preferred_element_type=jnp.float32).astype(jnp.bfloat16)
    mixed_all = lax.map(mixer_pass, streams)
    return jnp.concatenate([mixed_all[:BATCH], jnp.flip(mixed_all[BATCH:], -1)], -1)
```

```python
import jax
import jax.numpy as jnp
from jax import lax
from jax.experimental import pallas as pl
from jax.experimental.pallas import tpu as pltpu
from jax.sharding import PartitionSpec as P

INNER = 2048
HEADS = 32
STATE = 128
SPAN = 128
HEADDIM = 64
PAIRS = INNER // 128
CONVW = INNER + 2 * STATE
F32 = jnp.float32
BF16 = jnp.bfloat16
BIG = pltpu.CompilerParams(vmem_limit_bytes=48 * 1024 * 1024)


def cost(flops, moved, exps):
    return pl.CostEstimate(flops=int(flops), bytes_accessed=int(moved), transcendentals=int(exps))


def silu(x):
    return x / (1.0 + jnp.exp(-x))


def spread(cells, pair):
    rows = cells.shape[0]
    low = jnp.broadcast_to(cells[:, 2 * pair : 2 * pair + 1], (rows, 128))
    high = jnp.broadcast_to(cells[:, 2 * pair + 1 : 2 * pair + 2], (rows, 128))
    return jnp.where(lax.broadcasted_iota(jnp.int32, (rows, 128), 1) < HEADDIM, low, high)


def states_kernel(
    conv, before, after, weight, bias, scaled_f, scaled_b, growth_f, growth_b,
    act_f, act_b, states_f, states_b, total_f, total_b, pad,
):
    length = conv.shape[0]
    spans = length // SPAN

    @pl.loop(0, CONVW // 128)
    def _(j):
        cols = pl.ds(pl.multiple_of(j * 128, 128), 128)
        pad[0:8, :] = before[:, cols].astype(F32)
        pad[8 : 8 + length, :] = conv[:, cols].astype(F32)
        pad[8 + length : 16 + length, :] = after[:, cols].astype(F32)
        taps = [weight[k : k + 1, cols] for k in range(4)]
        start = bias[:, cols]
        for k in range(spans):
            base = k * SPAN + 5
            ahead = start
            behind = start
            for tap in range(4):
                ahead = ahead + taps[tap] * pad[base + tap : base + tap + SPAN, :]
                behind = behind + taps[tap] * pad[base + 6 - tap : base + 6 - tap + SPAN, :]
            act_f[k * SPAN : (k + 1) * SPAN, cols] = silu(ahead).astype(BF16)
            act_b[k * SPAN : (k + 1) * SPAN, cols] = silu(behind).astype(BF16)

    for act, scaled, growth, states, total, order in (
        (act_f, scaled_f, growth_f, states_f, total_f, range(spans)),
        (act_b, scaled_b, growth_b, states_b, total_b, range(spans - 1, -1, -1)),
    ):

        @pl.loop(0, spans)
        def _(k):
            rows = pl.ds(pl.multiple_of(k * SPAN, SPAN), SPAN)
            write = act[rows, INNER : INNER + STATE].astype(F32).T.astype(BF16)
            scale = scaled[rows, :]
            for group in range(PAIRS // 2):
                parts = []
                for pair in (2 * group, 2 * group + 1):
                    vals = act[rows, pair * 128 : (pair + 1) * 128].astype(F32)
                    parts.append((vals * spread(scale, pair)).astype(BF16))
                states[rows, group * 256 : (group + 1) * 256] = jnp.dot(
                    write, jnp.concatenate(parts, 1), preferred_element_type=F32
                )

        for pair in range(PAIRS):
            cols = slice(pair * 128, (pair + 1) * 128)
            running = None
            for k in order:
                fresh = states[k * SPAN : (k + 1) * SPAN, cols]
                running = fresh if running is None else growth[k : k + 1, cols] * running + fresh
            total[:, cols] = running


def within_kernel(act_f, act_b, cum_f, cum_b, row_f, row_b, row_dt, skip, y_f, y_b):
    down = lax.broadcasted_iota(jnp.int32, (SPAN, SPAN), 0)
    across = lax.broadcasted_iota(jnp.int32, (SPAN, SPAN), 1)
    low_lanes = across < HEADDIM
    for act, cum, row, out, causal in (
        (act_f, cum_f, row_f, y_f, down >= across),
        (act_b, cum_b, row_b, y_b, down <= across),
    ):
        write = act[:, INNER : INNER + STATE]
        read = act[:, INNER + STATE :]
        scores = lax.dot_general(
            read, write, (((1,), (1,)), ((), ())), preferred_element_type=F32
        )
        column = cum[...]
        for pair in range(PAIRS):
            mixes = []
            for head in (2 * pair, 2 * pair + 1):
                gap = column[:, head : head + 1] - row[head : head + 1, :]
                decay = jnp.exp(jnp.where(causal, gap, -jnp.inf))
                mixes.append((scores * decay * row_dt[head : head + 1, :]).astype(BF16))
            cols = slice(pair * 128, (pair + 1) * 128)
            vals = act[:, cols]
            wide = vals.astype(F32)
            apart = jnp.concatenate(
                [
                    jnp.where(low_lanes, wide, 0.0).astype(BF16),
                    jnp.where(low_lanes, 0.0, wide).astype(BF16),
                ],
                0,
            )
            inner = jnp.dot(jnp.concatenate(mixes, 1), apart, preferred_element_type=F32)
            out[:, cols] = inner + skip[:, cols] * wide


def finish_kernel(
    y_f, y_b, gate, read_f, read_b, cum_f, cum_b, states_f, states_b, in_f, in_b,
    growth_f, growth_b, gain, weight, turn, out, entry_f, entry_b, gated_f, gated_b, comb,
):
    step = pl.program_id(0)
    spans = entry_f.shape[0] // SPAN

    @pl.when(step == 0)
    def _():
        for states, start, growth, entry, order in (
            (states_f, in_f, growth_f, entry_f, range(spans)),
            (states_b, in_b, growth_b, entry_b, range(spans - 1, -1, -1)),
        ):
            for pair in range(PAIRS):
                cols = slice(pair * 128, (pair + 1) * 128)
                running = start[:, cols].astype(F32)
                for k in order:
                    rows = slice(k * SPAN, (k + 1) * SPAN)
                    entry[rows, cols] = running.astype(BF16)
                    running = growth[k : k + 1, cols] * running + states[rows, cols]

    rows = pl.ds(pl.multiple_of(step * SPAN, SPAN), SPAN)
    scales = []
    grown_f, grown_b = jnp.exp(cum_f[...]), jnp.exp(cum_b[...])
    square_f = jnp.zeros((SPAN, 128), F32)
    square_b = jnp.zeros((SPAN, 128), F32)
    for group in range(PAIRS // 2):
        wide = slice(group * 256, (group + 1) * 256)
        from_f = jnp.dot(read_f[...], entry_f[rows, wide], preferred_element_type=F32)
        from_b = jnp.dot(read_b[...], entry_b[rows, wide], preferred_element_type=F32)
        for half in range(2):
            pair = 2 * group + half
            cols = slice(pair * 128, (pair + 1) * 128)
            part = slice(half * 128, (half + 1) * 128)
            opened = silu(gate[:, cols].astype(F32))
            v_f = (y_f[:, cols] + from_f[:, part] * spread(grown_f, pair)) * opened
            v_b = (y_b[:, cols] + from_b[:, part] * spread(grown_b, pair)) * opened
            gated_f[:, cols] = v_f
            gated_b[:, cols] = v_b
            square_f += v_f * v_f
            square_b += v_b * v_b
    scale_f = lax.rsqrt(jnp.sum(square_f, 1, keepdims=True) / INNER + 1e-5)
    scale_b = lax.rsqrt(jnp.sum(square_b, 1, keepdims=True) / INNER + 1e-5)
    for pair in range(PAIRS):
        cols = slice(pair * 128, (pair + 1) * 128)
        both = gated_f[:, cols] * scale_f + gated_b[:, cols] * scale_b
        comb[:, cols] = (both * gain[:, cols]).astype(BF16)
    stream = jnp.dot(comb[...], weight[...], preferred_element_type=F32).astype(BF16)
    out[...] = jnp.dot(stream, turn[...], preferred_element_type=F32).astype(BF16)


def whole(*shape):
    return pl.BlockSpec(shape, lambda *_: (0,) * len(shape))


def on_device(
    hidden, in_weight, dt_weight, conv_weight, conv_bias, dt_bias, a_log, d_skip, norm_gain,
    out_weight,
):
    model = hidden.shape[2] // 2
    half = hidden.shape[1]
    length = 2 * half
    spans = length // SPAN
    count = lax.axis_size("seq")
    odd = lax.axis_index("seq") % 2 == 1
    swap = [(i, i ^ 1) for i in range(count)]
    up = [(i, i + 2) for i in range(count - 2)]
    down = [(i + 2, i) for i in range(count - 2)]

    weight = lax.all_gather(in_weight, "batch", axis=0, tiled=True)
    last_weight = lax.all_gather(out_weight, "batch", axis=0, tiled=True)

    ahead_half, reverse_half = hidden[0, :, :model], hidden[0, :, model:]
    kept = jnp.where(odd, reverse_half, ahead_half)
    got = lax.ppermute(jnp.where(odd, ahead_half, reverse_half), "seq", swap)
    rows = jnp.concatenate([jnp.where(odd, got, kept), jnp.where(odd, kept, got)], 0)
    a = lax.broadcasted_iota(jnp.int32, (model, model), 0)
    b = lax.broadcasted_iota(jnp.int32, (model, model), 1)
    turn = jnp.where(odd, a + b == model - 1, a == b).astype(BF16)
    stream = jnp.dot(rows, turn, preferred_element_type=F32).astype(BF16)

    step = jax.nn.softplus(
        jnp.dot(stream, dt_weight, preferred_element_type=F32) + dt_bias[None]
    )
    rates = (step * -jnp.exp(a_log)[None]).reshape(spans, SPAN, HEADS)
    place = jnp.arange(SPAN)
    lower = (place[:, None] >= place[None]).astype(F32)
    high = lax.Precision.HIGHEST
    cum_f = jnp.einsum("ts,ksh->kth", lower, rates, precision=high)
    cum_b = jnp.einsum("ts,ksh->kth", lower.T, rates, precision=high)
    end_f, end_b = cum_f[:, -1], cum_b[:, 0]
    step_spans = step.reshape(spans, SPAN, HEADS)
    scaled_f = (jnp.exp(end_f[:, None] - cum_f) * step_spans).reshape(length, HEADS)
    scaled_b = (jnp.exp(end_b[:, None] - cum_b) * step_spans).reshape(length, HEADS)
    growth_f = jnp.repeat(jnp.exp(end_f), HEADDIM, 1)
    growth_b = jnp.repeat(jnp.exp(end_b), HEADDIM, 1)
    cum_f, cum_b = cum_f.reshape(length, HEADS), cum_b.reshape(length, HEADS)
    row_f, row_b, row_dt = cum_f.T, cum_b.T, step.T

    projected = jnp.dot(stream, weight, preferred_element_type=F32).astype(BF16)
    conv_in = projected[:, INNER:]
    before = lax.ppermute(conv_in[-8:], "seq", up)
    after = lax.ppermute(conv_in[:8], "seq", down)

    like = jax.ShapeDtypeStruct
    act_f, act_b, states_f, states_b, total_f, total_b = pl.pallas_call(
        states_kernel,
        out_shape=[like((length, CONVW), BF16)] * 2
        + [like((length, INNER), F32)] * 2
        + [like((STATE, INNER), F32)] * 2,
        scratch_shapes=[pltpu.VMEM((length + 16, 128), F32)],
        compiler_params=BIG,
        cost_estimate=cost(8e9, 20e6, 3e6),
        name="states",
    )(
        conv_in, before, after, conv_weight, conv_bias[None], scaled_f, scaled_b, growth_f,
        growth_b,
    )

    def entering(total, growth, moves):
        decay = jnp.prod(growth, 0)[None]
        state = jnp.zeros((STATE, INNER), BF16)
        for lap in range(count // 2 - 1):
            outgoing = total if lap == 0 else total + decay * state.astype(F32)
            state = lax.ppermute(outgoing.astype(BF16), "seq", moves)
        return state

    in_f = entering(total_f, growth_f, up)
    in_b = entering(total_b, growth_b, down)

    def strip(width, at=0):
        return pl.BlockSpec((SPAN, width), lambda k: (k, at))

    def slab():
        return pl.BlockSpec((HEADS, SPAN), lambda k: (0, k))

    y_f, y_b = pl.pallas_call(
        within_kernel,
        grid=(spans,),
        in_specs=[strip(CONVW)] * 2 + [strip(HEADS)] * 2 + [slab()] * 3 + [whole(1, INNER)],
        out_specs=[strip(INNER)] * 2,
        out_shape=[like((length, INNER), F32)] * 2,
        compiler_params=BIG,
        cost_estimate=cost(25e9, 15e6, 5e6),
        name="within",
    )(act_f, act_b, cum_f, cum_b, row_f, row_b, row_dt, jnp.repeat(d_skip, HEADDIM)[None])

    out = pl.pallas_call(
        finish_kernel,
        grid=(spans,),
        in_specs=[strip(INNER)] * 2
        + [strip(INNER)]
        + [strip(STATE, CONVW // STATE - 1)] * 2
        + [strip(HEADS)] * 2
        + [whole(length, INNER)] * 2
        + [whole(STATE, INNER)] * 2
        + [whole(spans, INNER)] * 2
        + [whole(1, INNER), whole(INNER, model), whole(model, model)],
        out_specs=strip(model),
        out_shape=like((length, model), BF16),
        scratch_shapes=[pltpu.VMEM((length, INNER), BF16)] * 2
        + [pltpu.VMEM((SPAN, INNER), F32)] * 2
        + [pltpu.VMEM((SPAN, INNER), BF16)],
        compiler_params=BIG,
        cost_estimate=cost(8e9, 20e6, 2e6),
        name="finish",
    )(
        y_f, y_b, projected, act_f, act_b, cum_f, cum_b, states_f, states_b, in_f, in_b,
        growth_f, growth_b, norm_gain[None], last_weight, turn,
    )

    first, second = out[:half], out[half:]
    mine = jnp.where(odd, second, first)
    back = lax.ppermute(jnp.where(odd, first, second), "seq", swap)
    return jnp.concatenate([jnp.where(odd, back, mine), jnp.where(odd, mine, back)], 1)[None]


def solution(mesh):
    placed = (
        P("batch", "seq", None), P("batch", None), P(), P(), P(), P(), P(), P(), P(),
        P("batch", None),
    )
    return jax.shard_map(
        on_device, mesh=mesh, in_specs=placed, out_specs=P("batch", "seq", None), check_vma=False
    )
```

```python
import jax
import jax.numpy as jnp
from jax import lax
from jax.experimental import pallas as pl
from jax.experimental.pallas import tpu as pltpu
from jax.sharding import PartitionSpec as P

INNER = 2048
HEADS = 32
STATE = 128
SPAN = 128
HEADDIM = 64
PAIRS = INNER // 128
CONVW = INNER + 2 * STATE
EDGE = 16
CHUNKS = 8
PIECES = 4
MESH = pl.DeviceIdType.MESH
F32 = jnp.float32
BF16 = jnp.bfloat16
BIG = pltpu.CompilerParams(vmem_limit_bytes=48 * 1024 * 1024)


def cost(flops, moved, exps):
    return pl.CostEstimate(flops=int(flops), bytes_accessed=int(moved), transcendentals=int(exps))


def silu(x):
    return x / (1.0 + jnp.exp(-x))


def spread(cells, pair):
    rows = cells.shape[0]
    low = jnp.broadcast_to(cells[:, 2 * pair : 2 * pair + 1], (rows, 128))
    high = jnp.broadcast_to(cells[:, 2 * pair + 1 : 2 * pair + 2], (rows, 128))
    return jnp.where(lax.broadcasted_iota(jnp.int32, (rows, 128), 1) < HEADDIM, low, high)


def states_kernel(
    proj, weight, bias, scaled_f, scaled_b, growth_f, growth_b,
    act_f, act_b, states_f, states_b, total_f, total_b, pad,
):
    length = act_f.shape[0]
    spans = length // SPAN

    @pl.loop(0, CONVW // 128)
    def _(j):
        cols = pl.ds(pl.multiple_of(j * 128, 128), 128)
        source = pl.ds(pl.multiple_of(INNER + j * 128, 128), 128)
        pad[0:EDGE, :] = proj[length : length + EDGE, source].astype(F32)
        pad[EDGE : EDGE + length, :] = proj[0:length, source].astype(F32)
        pad[EDGE + length :, :] = proj[length + EDGE :, source].astype(F32)
        taps = [weight[k : k + 1, cols] for k in range(4)]
        start = bias[:, cols]
        for k in range(spans):
            base = k * SPAN + EDGE - 3
            ahead = start
            behind = start
            for tap in range(4):
                ahead = ahead + taps[tap] * pad[base + tap : base + tap + SPAN, :]
                behind = behind + taps[tap] * pad[base + 6 - tap : base + 6 - tap + SPAN, :]
            act_f[k * SPAN : (k + 1) * SPAN, cols] = silu(ahead).astype(BF16)
            act_b[k * SPAN : (k + 1) * SPAN, cols] = silu(behind).astype(BF16)

    for act, scaled, growth, states, total, order in (
        (act_f, scaled_f, growth_f, states_f, total_f, range(spans)),
        (act_b, scaled_b, growth_b, states_b, total_b, range(spans - 1, -1, -1)),
    ):

        @pl.loop(0, spans)
        def _(k):
            rows = pl.ds(pl.multiple_of(k * SPAN, SPAN), SPAN)
            write = act[rows, INNER : INNER + STATE].astype(F32).T.astype(BF16)
            scale = scaled[rows, :]
            for group in range(PAIRS // 2):
                parts = []
                for pair in (2 * group, 2 * group + 1):
                    vals = act[rows, pair * 128 : (pair + 1) * 128].astype(F32)
                    parts.append((vals * spread(scale, pair)).astype(BF16))
                states[rows, group * 256 : (group + 1) * 256] = jnp.dot(
                    write, jnp.concatenate(parts, 1), preferred_element_type=F32
                )

        for pair in range(PAIRS):
            cols = slice(pair * 128, (pair + 1) * 128)
            running = None
            for k in order:
                fresh = states[k * SPAN : (k + 1) * SPAN, cols]
                running = fresh if running is None else growth[k : k + 1, cols] * running + fresh
            total[:, cols] = running


def within_kernel(act_f, act_b, cum_f, cum_b, row_f, row_b, row_dt, skip, y_f, y_b):
    down = lax.broadcasted_iota(jnp.int32, (SPAN, SPAN), 0)
    across = lax.broadcasted_iota(jnp.int32, (SPAN, SPAN), 1)
    low_lanes = across < HEADDIM
    for act, cum, row, out, causal in (
        (act_f, cum_f, row_f, y_f, down >= across),
        (act_b, cum_b, row_b, y_b, down <= across),
    ):
        write = act[:, INNER : INNER + STATE]
        read = act[:, INNER + STATE :]
        scores = lax.dot_general(
            read, write, (((1,), (1,)), ((), ())), preferred_element_type=F32
        )
        column = cum[...]
        for pair in range(PAIRS):
            mixes = []
            for head in (2 * pair, 2 * pair + 1):
                gap = column[:, head : head + 1] - row[head : head + 1, :]
                decay = jnp.exp(jnp.where(causal, gap, -jnp.inf))
                mixes.append((scores * decay * row_dt[head : head + 1, :]).astype(BF16))
            cols = slice(pair * 128, (pair + 1) * 128)
            vals = act[:, cols]
            wide = vals.astype(F32)
            apart = jnp.concatenate(
                [
                    jnp.where(low_lanes, wide, 0.0).astype(BF16),
                    jnp.where(low_lanes, 0.0, wide).astype(BF16),
                ],
                0,
            )
            inner = jnp.dot(jnp.concatenate(mixes, 1), apart, preferred_element_type=F32)
            out[:, cols] = inner + skip[:, cols] * wide


def finish_kernel(
    y_f, y_b, gate, read_f, read_b, cum_f, cum_b, states_f, states_b, in_f, in_b,
    growth_f, growth_b, gain, weight, turn, out, entry_f, entry_b, gated_f, gated_b, comb,
):
    step = pl.program_id(0)
    spans = entry_f.shape[0] // SPAN

    @pl.when(step == 0)
    def _():
        for states, start, growth, entry, order in (
            (states_f, in_f, growth_f, entry_f, range(spans)),
            (states_b, in_b, growth_b, entry_b, range(spans - 1, -1, -1)),
        ):
            for pair in range(PAIRS):
                cols = slice(pair * 128, (pair + 1) * 128)
                running = start[:, cols].astype(F32)
                for k in order:
                    rows = slice(k * SPAN, (k + 1) * SPAN)
                    entry[rows, cols] = running.astype(BF16)
                    running = growth[k : k + 1, cols] * running + states[rows, cols]

    rows = pl.ds(pl.multiple_of(step * SPAN, SPAN), SPAN)
    scales = []
    grown_f, grown_b = jnp.exp(cum_f[...]), jnp.exp(cum_b[...])
    square_f = jnp.zeros((SPAN, 128), F32)
    square_b = jnp.zeros((SPAN, 128), F32)
    for group in range(PAIRS // 2):
        wide = slice(group * 256, (group + 1) * 256)
        from_f = jnp.dot(read_f[...], entry_f[rows, wide], preferred_element_type=F32)
        from_b = jnp.dot(read_b[...], entry_b[rows, wide], preferred_element_type=F32)
        for half in range(2):
            pair = 2 * group + half
            cols = slice(pair * 128, (pair + 1) * 128)
            part = slice(half * 128, (half + 1) * 128)
            opened = silu(gate[:, cols].astype(F32))
            v_f = (y_f[:, cols] + from_f[:, part] * spread(grown_f, pair)) * opened
            v_b = (y_b[:, cols] + from_b[:, part] * spread(grown_b, pair)) * opened
            gated_f[:, cols] = v_f
            gated_b[:, cols] = v_b
            square_f += v_f * v_f
            square_b += v_b * v_b
    scale_f = lax.rsqrt(jnp.sum(square_f, 1, keepdims=True) / INNER + 1e-5)
    scale_b = lax.rsqrt(jnp.sum(square_b, 1, keepdims=True) / INNER + 1e-5)
    for pair in range(PAIRS):
        cols = slice(pair * 128, (pair + 1) * 128)
        both = gated_f[:, cols] * scale_f + gated_b[:, cols] * scale_b
        comb[:, cols] = (both * gain[:, cols]).astype(BF16)
    stream = jnp.dot(comb[...], weight[...], preferred_element_type=F32).astype(BF16)
    out[...] = jnp.dot(stream, turn[...], preferred_element_type=F32).astype(BF16)


def collect_kernel(hidden, shard, rows, weight, blank, local, swap, halo, ysem, zsem, csem, osem):
    place, part = lax.axis_index("seq"), lax.axis_index("batch")
    count = lax.axis_size("seq")
    odd = place % 2
    upper = (place // 2) % 2
    half, model = hidden.shape[1], hidden.shape[2] // 2
    depth = shard.shape[0]
    piece = depth // 2 // CHUNKS
    beside = (place + 1 - 2 * odd, part)
    along = (place + 2 - 4 * upper, part)
    across = (place, (part + 2) % 4)
    core = (place, part + 1 - 2 * (part % 2))
    slant = place - 1 + 2 * odd

    barrier = pltpu.get_barrier_semaphore()

    def greet(device):
        pl.semaphore_signal(barrier, inc=1, device_id=device, device_id_type=MESH)

    for device in (beside, across, core):
        greet(device)
    lower_there, upper_there = place >= 2, place + 2 < count
    slant_there = (slant >= 0) & (slant < count)

    for there, seat in ((lower_there, place - 2), (upper_there, place + 2), (slant_there, slant)):

        @pl.when(there)
        def _(seat=seat):
            greet((seat, part))

    others = [there.astype(jnp.int32) for there in (lower_there, upper_there, slant_there)]
    pl.semaphore_wait(barrier, 3 + sum(others))

    def remote(src, dst, sems, at, device):
        return pltpu.make_async_remote_copy(
            src_ref=src, dst_ref=dst, send_sem=sems.at[0, at], recv_sem=sems.at[1, at],
            device_id=device, device_id_type=MESH,
        )

    def mine(i, side):
        return shard.at[pl.ds(pl.multiple_of(side * (depth // 2) + i * piece, 16), piece)]

    def slot(owner, i, side):
        at = owner * depth + side * (depth // 2) + i * piece
        return weight.at[pl.ds(pl.multiple_of(at, 16), piece)]

    def whole_slot(owner):
        return weight.at[pl.ds(pl.multiple_of(owner * depth, 16), depth)]

    far = (part + 2) % 4
    over_y = [remote(mine(i, upper), slot(part, i, upper), ysem, i, across) for i in range(CHUNKS)]
    for copy in over_y:
        copy.start()
    spot = rows.at[pl.ds(pl.multiple_of(odd * half, 16), half)]
    kept_cols = pl.ds(pl.multiple_of(odd * model, 128), model)
    sent_cols = pl.ds(pl.multiple_of((1 - odd) * model, 128), model)
    swapping = remote(hidden.at[0, :, sent_cols], spot, swap, 0, beside)
    swapping.start()
    own_core = remote(shard, whole_slot(part), osem, 0, core)
    own_core.start()
    own = pltpu.make_async_copy(shard, whole_slot(part), local.at[0])
    own.start()
    kept = pltpu.make_async_copy(hidden.at[0, :, kept_cols], spot, local.at[1])
    kept.start()

    before = rows.at[pl.ds(2 * half, EDGE)]
    after = rows.at[pl.ds(2 * half + EDGE, EDGE)]
    last, first = pl.ds(half - EDGE, EDGE), pl.ds(0, EDGE)
    low_cols, high_cols = pl.ds(0, model), pl.ds(model, model)
    halos = [
        ((odd == 1) & upper_there, hidden.at[0, last, high_cols], before, 0, place + 2),
        ((odd == 1) & slant_there, hidden.at[0, last, low_cols], before, 0, place + 1),
        ((odd == 0) & lower_there, hidden.at[0, first, low_cols], after, 1, place - 2),
        ((odd == 0) & slant_there, hidden.at[0, first, high_cols], after, 1, place - 1),
    ]

    def halo_copy(at):
        there, src, dst, kind, seat = halos[at]
        return there, pltpu.make_async_remote_copy(
            src_ref=src, dst_ref=dst, send_sem=halo.at[0, at], recv_sem=halo.at[1, kind],
            device_id=(seat, part), device_id_type=MESH,
        )

    for at in range(4):
        there, copy = halo_copy(at)

        @pl.when(there)
        def _(copy=copy):
            copy.start()

    blank[...] = jnp.zeros_like(blank)
    pair_last = count // 2 - 1
    for missing, dst, at in ((place // 2 == 0, before, 2), (place // 2 == pair_last, after, 3)):

        @pl.when(missing)
        def _(dst=dst, at=at):
            fill = pltpu.make_async_copy(blank, dst, local.at[at])
            fill.start()
            fill.wait()

    on_z = [remote(slot(far, i, upper), slot(far, i, upper), zsem, i, along) for i in range(CHUNKS)]
    first_core = [
        remote(slot(far, i, upper), slot(far, i, upper), csem, i, core) for i in range(CHUNKS)
    ]
    from_z = [
        remote(slot(far, i, 1 - upper), slot(far, i, 1 - upper), zsem, i, along)
        for i in range(CHUNKS)
    ]
    second_core = [
        remote(slot(far, i, 1 - upper), slot(far, i, 1 - upper), csem, CHUNKS + i, core)
        for i in range(CHUNKS)
    ]
    for i in range(CHUNKS + 1):
        if i < CHUNKS:
            over_y[i].wait_recv()
            on_z[i].start()
            first_core[i].start()
        if i > 0:
            from_z[i - 1].wait_recv()
            second_core[i - 1].start()
    for i in range(CHUNKS):
        over_y[i].wait_send()
        on_z[i].wait_send()
        first_core[i].wait()
        second_core[i].wait()
    own.wait()
    kept.wait()
    own_core.wait()
    swapping.wait()
    for at in range(4):
        there, copy = halo_copy(at)

        @pl.when(there)
        def _(copy=copy):
            copy.wait_send()

    for there, dst, kind in ((place // 2 > 0, before, 0), (place // 2 < pair_last, after, 1)):

        @pl.when(there)
        def _(dst=dst, kind=kind):
            pltpu.make_async_remote_copy(
                src_ref=dst, dst_ref=dst, send_sem=halo.at[0, kind], recv_sem=halo.at[1, kind],
                device_id=beside, device_id_type=MESH,
            ).wait_recv()


def chain_kernel(total_f, total_b, decay_f, decay_b, in_f, in_b, out_f, out_b, land_f, land_b, fsem, bsem):
    place, part = lax.axis_index("seq"), lax.axis_index("batch")
    count = lax.axis_size("seq")
    lower_there, upper_there = place >= 2, place + 2 < count
    barrier = pltpu.get_barrier_semaphore()
    for there, seat in ((lower_there, place - 2), (upper_there, place + 2)):

        @pl.when(there)
        def _(seat=seat):
            pl.semaphore_signal(barrier, inc=1, device_id=(seat, part), device_id_type=MESH)

    pl.semaphore_wait(barrier, lower_there.astype(jnp.int32) + upper_there.astype(jnp.int32))

    width = total_f.shape[1] // PIECES
    ways = (
        (total_f, decay_f, in_f, out_f, land_f, fsem, lower_there, upper_there, place + 2),
        (total_b, decay_b, in_b, out_b, land_b, bsem, upper_there, lower_there, place - 2),
    )

    def hop(way, piece):
        _, _, _, out, land, sems, _, _, seat = way
        return pltpu.make_async_remote_copy(
            src_ref=out.at[piece], dst_ref=land.at[piece], send_sem=sems.at[0, piece],
            recv_sem=sems.at[1, piece], device_id=(seat, part), device_id_type=MESH,
        )

    for piece in range(PIECES):
        cols = slice(piece * width, (piece + 1) * width)
        for way in ways:
            total, decay, entry, out, land, sems, source, target, seat = way

            @pl.when(source)
            def _():
                hop(way, piece).wait_recv()
                state = land[piece]
                entry[:, cols] = state
                out[piece] = (total[:, cols] + decay[:, cols] * state.astype(F32)).astype(BF16)

            @pl.when(jnp.logical_not(source))
            def _():
                entry[:, cols] = jnp.zeros((STATE, width), BF16)
                out[piece] = total[:, cols].astype(BF16)

            @pl.when(target)
            def _():
                hop(way, piece).start()

    for piece in range(PIECES):
        for way in ways:

            @pl.when(way[7])
            def _():
                hop(way, piece).wait_send()


def whole(*shape):
    return pl.BlockSpec(shape, lambda *_: (0,) * len(shape))


def on_device(
    hidden, in_weight, dt_weight, conv_weight, conv_bias, dt_bias, a_log, d_skip, norm_gain,
    out_weight,
):
    model = hidden.shape[2] // 2
    half = hidden.shape[1]
    length = 2 * half
    spans = length // SPAN
    count = lax.axis_size("seq")
    odd = lax.axis_index("seq") % 2 == 1
    swap = [(i, i ^ 1) for i in range(count)]

    like = jax.ShapeDtypeStruct
    anywhere = pl.BlockSpec(memory_space=pl.ANY)
    dma = pltpu.SemaphoreType.DMA
    rows, weight = pl.pallas_call(
        collect_kernel,
        in_specs=[anywhere] * 2,
        out_specs=[anywhere] * 2,
        out_shape=[
            like((length + 2 * EDGE, model), BF16),
            like((4 * in_weight.shape[0], in_weight.shape[1]), BF16),
        ],
        scratch_shapes=[
            pltpu.VMEM((EDGE, model), BF16), dma((4,)), dma((2, 1)), dma((2, 4)),
            dma((2, CHUNKS)), dma((2, CHUNKS)), dma((2, 2 * CHUNKS)), dma((2, 1)),
        ],
        compiler_params=pltpu.CompilerParams(collective_id=0, has_side_effects=True),
        cost_estimate=cost(0, 20e6, 0),
        name="collect",
    )(hidden, in_weight)
    out_weight, weight = lax.optimization_barrier((out_weight, weight))
    last_weight = lax.all_gather(out_weight, "batch", axis=0, tiled=True)

    a = lax.broadcasted_iota(jnp.int32, (model, model), 0)
    b = lax.broadcasted_iota(jnp.int32, (model, model), 1)
    turn = jnp.where(odd, a + b == model - 1, a == b).astype(BF16)
    stream = jnp.dot(rows, turn, preferred_element_type=F32).astype(BF16)

    step = jax.nn.softplus(
        jnp.dot(stream[:length], dt_weight, preferred_element_type=F32) + dt_bias[None]
    )
    rates = (step * -jnp.exp(a_log)[None]).reshape(spans, SPAN, HEADS)
    place = jnp.arange(SPAN)
    lower = (place[:, None] >= place[None]).astype(F32)
    high = lax.Precision.HIGHEST
    cum_f = jnp.einsum("ts,ksh->kth", lower, rates, precision=high)
    cum_b = jnp.einsum("ts,ksh->kth", lower.T, rates, precision=high)
    end_f, end_b = cum_f[:, -1], cum_b[:, 0]
    step_spans = step.reshape(spans, SPAN, HEADS)
    scaled_f = (jnp.exp(end_f[:, None] - cum_f) * step_spans).reshape(length, HEADS)
    scaled_b = (jnp.exp(end_b[:, None] - cum_b) * step_spans).reshape(length, HEADS)
    growth_f = jnp.repeat(jnp.exp(end_f), HEADDIM, 1)
    growth_b = jnp.repeat(jnp.exp(end_b), HEADDIM, 1)
    cum_f, cum_b = cum_f.reshape(length, HEADS), cum_b.reshape(length, HEADS)
    row_f, row_b, row_dt = cum_f.T, cum_b.T, step.T

    projected = jnp.dot(stream, weight, preferred_element_type=F32).astype(BF16)
    act_f, act_b, states_f, states_b, total_f, total_b = pl.pallas_call(
        states_kernel,
        out_shape=[like((length, CONVW), BF16)] * 2
        + [like((length, INNER), F32)] * 2
        + [like((STATE, INNER), F32)] * 2,
        scratch_shapes=[pltpu.VMEM((length + 2 * EDGE, 128), F32)],
        compiler_params=BIG,
        cost_estimate=cost(8e9, 20e6, 3e6),
        name="states",
    )(
        projected, conv_weight, conv_bias[None], scaled_f, scaled_b, growth_f, growth_b,
    )

    in_f, in_b = pl.pallas_call(
        chain_kernel,
        out_shape=[like((STATE, INNER), BF16)] * 2,
        scratch_shapes=[pltpu.VMEM((PIECES, STATE, INNER // PIECES), BF16)] * 4
        + [dma((2, PIECES))] * 2,
        compiler_params=pltpu.CompilerParams(
            collective_id=1, has_side_effects=True, vmem_limit_bytes=32 * 1024 * 1024
        ),
        cost_estimate=cost(2e6, 8e6, 0),
        name="chain",
    )(total_f, total_b, jnp.prod(growth_f, 0)[None], jnp.prod(growth_b, 0)[None])

    def strip(width, at=0):
        return pl.BlockSpec((SPAN, width), lambda k: (k, at))

    def slab():
        return pl.BlockSpec((HEADS, SPAN), lambda k: (0, k))

    y_f, y_b = pl.pallas_call(
        within_kernel,
        grid=(spans,),
        in_specs=[strip(CONVW)] * 2 + [strip(HEADS)] * 2 + [slab()] * 3 + [whole(1, INNER)],
        out_specs=[strip(INNER)] * 2,
        out_shape=[like((length, INNER), F32)] * 2,
        compiler_params=BIG,
        cost_estimate=cost(25e9, 15e6, 5e6),
        name="within",
    )(act_f, act_b, cum_f, cum_b, row_f, row_b, row_dt, jnp.repeat(d_skip, HEADDIM)[None])

    out = pl.pallas_call(
        finish_kernel,
        grid=(spans,),
        in_specs=[strip(INNER)] * 2
        + [strip(INNER)]
        + [strip(STATE, CONVW // STATE - 1)] * 2
        + [strip(HEADS)] * 2
        + [whole(length, INNER)] * 2
        + [whole(STATE, INNER)] * 2
        + [whole(spans, INNER)] * 2
        + [whole(1, INNER), whole(INNER, model), whole(model, model)],
        out_specs=strip(model),
        out_shape=like((length, model), BF16),
        scratch_shapes=[pltpu.VMEM((length, INNER), BF16)] * 2
        + [pltpu.VMEM((SPAN, INNER), F32)] * 2
        + [pltpu.VMEM((SPAN, INNER), BF16)],
        compiler_params=BIG,
        cost_estimate=cost(8e9, 20e6, 2e6),
        name="finish",
    )(
        y_f, y_b, projected, act_f, act_b, cum_f, cum_b, states_f, states_b, in_f, in_b,
        growth_f, growth_b, norm_gain[None], last_weight, turn,
    )

    first, second = out[:half], out[half:]
    mine = jnp.where(odd, second, first)
    back = lax.ppermute(jnp.where(odd, first, second), "seq", swap)
    return jnp.concatenate([jnp.where(odd, back, mine), jnp.where(odd, mine, back)], 1)[None]


def solution(mesh):
    placed = (
        P("batch", "seq", None), P("batch", None), P(), P(), P(), P(), P(), P(), P(),
        P("batch", None),
    )
    return jax.shard_map(
        on_device, mesh=mesh, in_specs=placed, out_specs=P("batch", "seq", None), check_vma=False
    )
```

```python
import jax
import jax.numpy as jnp
from jax import lax
from jax.experimental import pallas as pl
from jax.experimental.pallas import tpu as pltpu
from jax.sharding import PartitionSpec as P

INNER = 2048
HEADS = 32
STATE = 128
SPAN = 128
HEADDIM = 64
PAIRS = INNER // 128
CONVW = INNER + 2 * STATE
EDGE = 16
PIECES = 4
MESH = pl.DeviceIdType.MESH
F32 = jnp.float32
BF16 = jnp.bfloat16
BIG = pltpu.CompilerParams(vmem_limit_bytes=48 * 1024 * 1024)


def cost(flops, moved, exps):
    return pl.CostEstimate(flops=int(flops), bytes_accessed=int(moved), transcendentals=int(exps))


def silu(x):
    return x / (1.0 + jnp.exp(-x))


def spread(cells, pair):
    rows = cells.shape[0]
    low = jnp.broadcast_to(cells[:, 2 * pair : 2 * pair + 1], (rows, 128))
    high = jnp.broadcast_to(cells[:, 2 * pair + 1 : 2 * pair + 2], (rows, 128))
    return jnp.where(lax.broadcasted_iota(jnp.int32, (rows, 128), 1) < HEADDIM, low, high)


def states_kernel(
    proj, weight, bias, scaled_f, scaled_b, growth_f, growth_b,
    act_f, act_b, states_f, states_b, total_f, total_b, pad,
):
    length = act_f.shape[0]
    spans = length // SPAN

    @pl.loop(0, CONVW // 128)
    def _(j):
        cols = pl.ds(pl.multiple_of(j * 128, 128), 128)
        source = pl.ds(pl.multiple_of(INNER + j * 128, 128), 128)
        pad[0:EDGE, :] = proj[length : length + EDGE, source].astype(F32)
        pad[EDGE : EDGE + length, :] = proj[0:length, source].astype(F32)
        pad[EDGE + length :, :] = proj[length + EDGE :, source].astype(F32)
        taps = [weight[k : k + 1, cols] for k in range(4)]
        start = bias[:, cols]
        for k in range(spans):
            base = k * SPAN + EDGE - 3
            ahead = start
            behind = start
            for tap in range(4):
                ahead = ahead + taps[tap] * pad[base + tap : base + tap + SPAN, :]
                behind = behind + taps[tap] * pad[base + 6 - tap : base + 6 - tap + SPAN, :]
            act_f[k * SPAN : (k + 1) * SPAN, cols] = silu(ahead).astype(BF16)
            act_b[k * SPAN : (k + 1) * SPAN, cols] = silu(behind).astype(BF16)

    for act, scaled, growth, states, total, order in (
        (act_f, scaled_f, growth_f, states_f, total_f, range(spans)),
        (act_b, scaled_b, growth_b, states_b, total_b, range(spans - 1, -1, -1)),
    ):

        @pl.loop(0, spans)
        def _(k):
            rows = pl.ds(pl.multiple_of(k * SPAN, SPAN), SPAN)
            write = act[rows, INNER : INNER + STATE].astype(F32).T.astype(BF16)
            scale = scaled[rows, :]
            for group in range(PAIRS // 2):
                parts = []
                for pair in (2 * group, 2 * group + 1):
                    vals = act[rows, pair * 128 : (pair + 1) * 128].astype(F32)
                    parts.append((vals * spread(scale, pair)).astype(BF16))
                states[rows, group * 256 : (group + 1) * 256] = jnp.dot(
                    write, jnp.concatenate(parts, 1), preferred_element_type=F32
                )

        for pair in range(PAIRS):
            cols = slice(pair * 128, (pair + 1) * 128)
            running = None
            for k in order:
                fresh = states[k * SPAN : (k + 1) * SPAN, cols]
                running = fresh if running is None else growth[k : k + 1, cols] * running + fresh
            total[:, cols] = running


def within_kernel(act_f, act_b, cum_f, cum_b, row_f, row_b, row_dt, skip, y_f, y_b):
    down = lax.broadcasted_iota(jnp.int32, (SPAN, SPAN), 0)
    across = lax.broadcasted_iota(jnp.int32, (SPAN, SPAN), 1)
    low_lanes = across < HEADDIM
    for act, cum, row, out, causal in (
        (act_f, cum_f, row_f, y_f, down >= across),
        (act_b, cum_b, row_b, y_b, down <= across),
    ):
        write = act[:, INNER : INNER + STATE]
        read = act[:, INNER + STATE :]
        scores = lax.dot_general(
            read, write, (((1,), (1,)), ((), ())), preferred_element_type=F32
        )
        column = cum[...]
        for pair in range(PAIRS):
            mixes = []
            for head in (2 * pair, 2 * pair + 1):
                gap = column[:, head : head + 1] - row[head : head + 1, :]
                decay = jnp.exp(jnp.where(causal, gap, -jnp.inf))
                mixes.append((scores * decay * row_dt[head : head + 1, :]).astype(BF16))
            cols = slice(pair * 128, (pair + 1) * 128)
            vals = act[:, cols]
            wide = vals.astype(F32)
            apart = jnp.concatenate(
                [
                    jnp.where(low_lanes, wide, 0.0).astype(BF16),
                    jnp.where(low_lanes, 0.0, wide).astype(BF16),
                ],
                0,
            )
            inner = jnp.dot(jnp.concatenate(mixes, 1), apart, preferred_element_type=F32)
            out[:, cols] = inner + skip[:, cols] * wide


def finish_kernel(
    y_f, y_b, gate, read_f, read_b, cum_f, cum_b, states_f, states_b, in_f, in_b,
    growth_f, growth_b, gain, weight, turn, out, entry_f, entry_b, gated_f, gated_b, comb,
):
    step = pl.program_id(0)
    spans = entry_f.shape[0] // SPAN

    @pl.when(step == 0)
    def _():
        for states, start, growth, entry, order in (
            (states_f, in_f, growth_f, entry_f, range(spans)),
            (states_b, in_b, growth_b, entry_b, range(spans - 1, -1, -1)),
        ):
            for pair in range(PAIRS):
                cols = slice(pair * 128, (pair + 1) * 128)
                running = start[:, cols].astype(F32)
                for k in order:
                    rows = slice(k * SPAN, (k + 1) * SPAN)
                    entry[rows, cols] = running.astype(BF16)
                    running = growth[k : k + 1, cols] * running + states[rows, cols]

    rows = pl.ds(pl.multiple_of(step * SPAN, SPAN), SPAN)
    scales = []
    grown_f, grown_b = jnp.exp(cum_f[...]), jnp.exp(cum_b[...])
    square_f = jnp.zeros((SPAN, 128), F32)
    square_b = jnp.zeros((SPAN, 128), F32)
    for group in range(PAIRS // 2):
        wide = slice(group * 256, (group + 1) * 256)
        from_f = jnp.dot(read_f[...], entry_f[rows, wide], preferred_element_type=F32)
        from_b = jnp.dot(read_b[...], entry_b[rows, wide], preferred_element_type=F32)
        for half in range(2):
            pair = 2 * group + half
            cols = slice(pair * 128, (pair + 1) * 128)
            part = slice(half * 128, (half + 1) * 128)
            opened = silu(gate[:, cols].astype(F32))
            v_f = (y_f[:, cols] + from_f[:, part] * spread(grown_f, pair)) * opened
            v_b = (y_b[:, cols] + from_b[:, part] * spread(grown_b, pair)) * opened
            gated_f[:, cols] = v_f
            gated_b[:, cols] = v_b
            square_f += v_f * v_f
            square_b += v_b * v_b
    scale_f = lax.rsqrt(jnp.sum(square_f, 1, keepdims=True) / INNER + 1e-5)
    scale_b = lax.rsqrt(jnp.sum(square_b, 1, keepdims=True) / INNER + 1e-5)
    for pair in range(PAIRS):
        cols = slice(pair * 128, (pair + 1) * 128)
        both = gated_f[:, cols] * scale_f + gated_b[:, cols] * scale_b
        comb[:, cols] = (both * gain[:, cols]).astype(BF16)
    stream = jnp.dot(comb[...], weight[...], preferred_element_type=F32).astype(BF16)
    out[...] = jnp.dot(stream, turn[...], preferred_element_type=F32).astype(BF16)


def chain_kernel(total_f, total_b, decay_f, decay_b, in_f, in_b, out_f, out_b, land_f, land_b, fsem, bsem):
    place, part = lax.axis_index("seq"), lax.axis_index("batch")
    count = lax.axis_size("seq")
    lower_there, upper_there = place >= 2, place + 2 < count
    barrier = pltpu.get_barrier_semaphore()
    for there, seat in ((lower_there, place - 2), (upper_there, place + 2)):

        @pl.when(there)
        def _(seat=seat):
            pl.semaphore_signal(barrier, inc=1, device_id=(seat, part), device_id_type=MESH)

    pl.semaphore_wait(barrier, lower_there.astype(jnp.int32) + upper_there.astype(jnp.int32))

    width = total_f.shape[1] // PIECES
    ways = (
        (total_f, decay_f, in_f, out_f, land_f, fsem, lower_there, upper_there, place + 2),
        (total_b, decay_b, in_b, out_b, land_b, bsem, upper_there, lower_there, place - 2),
    )

    def hop(way, piece):
        _, _, _, out, land, sems, _, _, seat = way
        return pltpu.make_async_remote_copy(
            src_ref=out.at[piece], dst_ref=land.at[piece], send_sem=sems.at[0, piece],
            recv_sem=sems.at[1, piece], device_id=(seat, part), device_id_type=MESH,
        )

    def begin(way):
        total, _, entry, out, _, _, source, target, _ = way

        @pl.when(jnp.logical_not(source))
        def _():
            for piece in range(PIECES):
                cols = slice(piece * width, (piece + 1) * width)
                out[piece] = total[:, cols].astype(BF16)
                hop(way, piece).start()
                entry[:, cols] = jnp.zeros((STATE, width), BF16)

    def relay(way, piece):
        total, decay, entry, out, land, _, source, target, _ = way
        cols = slice(piece * width, (piece + 1) * width)

        @pl.when(source)
        def _():
            hop(way, piece).wait_recv()

            @pl.when(target)
            def _():
                passed = decay[:, cols] * land[piece].astype(F32)
                out[piece] = (total[:, cols] + passed).astype(BF16)
                hop(way, piece).start()

            entry[:, cols] = land[piece]

    for way in ways:
        begin(way)

    nearer = place < count // 2
    for near, order in ((nearer, ways), (jnp.logical_not(nearer), ways[::-1])):

        @pl.when(near)
        def _(order=order):
            for piece in range(PIECES):
                for way in order:
                    relay(way, piece)

    for piece in range(PIECES):
        for way in ways:

            @pl.when(way[7])
            def _():
                hop(way, piece).wait_send()


def whole(*shape):
    return pl.BlockSpec(shape, lambda *_: (0,) * len(shape))


def on_device(
    hidden, in_weight, dt_weight, conv_weight, conv_bias, dt_bias, a_log, d_skip, norm_gain,
    out_weight,
):
    model = hidden.shape[2] // 2
    half = hidden.shape[1]
    length = 2 * half
    spans = length // SPAN
    count = lax.axis_size("seq")
    odd = lax.axis_index("seq") % 2 == 1
    swap = [(i, i ^ 1) for i in range(count)]

    like = jax.ShapeDtypeStruct
    dma = pltpu.SemaphoreType.DMA
    up = [(i, i + 2) for i in range(count - 2)]
    down = [(i + 2, i) for i in range(count - 2)]
    weight = lax.all_gather(in_weight, "batch", axis=0, tiled=True)
    last_weight = lax.all_gather(out_weight, "batch", axis=0, tiled=True)

    ahead_half, reverse_half = hidden[0, :, :model], hidden[0, :, model:]
    kept = jnp.where(odd, reverse_half, ahead_half)
    got = lax.ppermute(jnp.where(odd, ahead_half, reverse_half), "seq", swap)
    early, late = jnp.where(odd, got, kept), jnp.where(odd, kept, got)
    before = lax.ppermute(late[-EDGE:], "seq", up)
    after = lax.ppermute(early[:EDGE], "seq", down)
    rows = jnp.concatenate([early, late, before, after], 0)

    a = lax.broadcasted_iota(jnp.int32, (model, model), 0)
    b = lax.broadcasted_iota(jnp.int32, (model, model), 1)
    turn = jnp.where(odd, a + b == model - 1, a == b).astype(BF16)
    stream = jnp.dot(rows, turn, preferred_element_type=F32).astype(BF16)

    step = jax.nn.softplus(
        jnp.dot(stream[:length], dt_weight, preferred_element_type=F32) + dt_bias[None]
    )
    rates = (step * -jnp.exp(a_log)[None]).reshape(spans, SPAN, HEADS)
    place = jnp.arange(SPAN)
    lower = (place[:, None] >= place[None]).astype(F32)
    high = lax.Precision.HIGHEST
    cum_f = jnp.einsum("ts,ksh->kth", lower, rates, precision=high)
    cum_b = jnp.einsum("ts,ksh->kth", lower.T, rates, precision=high)
    end_f, end_b = cum_f[:, -1], cum_b[:, 0]
    step_spans = step.reshape(spans, SPAN, HEADS)
    scaled_f = (jnp.exp(end_f[:, None] - cum_f) * step_spans).reshape(length, HEADS)
    scaled_b = (jnp.exp(end_b[:, None] - cum_b) * step_spans).reshape(length, HEADS)
    growth_f = jnp.repeat(jnp.exp(end_f), HEADDIM, 1)
    growth_b = jnp.repeat(jnp.exp(end_b), HEADDIM, 1)
    cum_f, cum_b = cum_f.reshape(length, HEADS), cum_b.reshape(length, HEADS)
    row_f, row_b, row_dt = cum_f.T, cum_b.T, step.T

    projected = jnp.dot(stream, weight, preferred_element_type=F32).astype(BF16)
    act_f, act_b, states_f, states_b, total_f, total_b = pl.pallas_call(
        states_kernel,
        out_shape=[like((length, CONVW), BF16)] * 2
        + [like((length, INNER), F32)] * 2
        + [like((STATE, INNER), F32)] * 2,
        scratch_shapes=[pltpu.VMEM((length + 2 * EDGE, 128), F32)],
        compiler_params=BIG,
        cost_estimate=cost(8e9, 20e6, 3e6),
        name="states",
    )(
        projected, conv_weight, conv_bias[None], scaled_f, scaled_b, growth_f, growth_b,
    )

    in_f, in_b = pl.pallas_call(
        chain_kernel,
        out_shape=[like((STATE, INNER), BF16)] * 2,
        scratch_shapes=[pltpu.VMEM((PIECES, STATE, INNER // PIECES), BF16)] * 4
        + [dma((2, PIECES))] * 2,
        compiler_params=pltpu.CompilerParams(
            collective_id=1, has_side_effects=True, vmem_limit_bytes=32 * 1024 * 1024
        ),
        cost_estimate=cost(2e6, 8e6, 0),
        name="chain",
    )(total_f, total_b, jnp.prod(growth_f, 0)[None], jnp.prod(growth_b, 0)[None])

    def strip(width, at=0):
        return pl.BlockSpec((SPAN, width), lambda k: (k, at))

    def slab():
        return pl.BlockSpec((HEADS, SPAN), lambda k: (0, k))

    y_f, y_b = pl.pallas_call(
        within_kernel,
        grid=(spans,),
        in_specs=[strip(CONVW)] * 2 + [strip(HEADS)] * 2 + [slab()] * 3 + [whole(1, INNER)],
        out_specs=[strip(INNER)] * 2,
        out_shape=[like((length, INNER), F32)] * 2,
        compiler_params=BIG,
        cost_estimate=cost(25e9, 15e6, 5e6),
        name="within",
    )(act_f, act_b, cum_f, cum_b, row_f, row_b, row_dt, jnp.repeat(d_skip, HEADDIM)[None])

    out = pl.pallas_call(
        finish_kernel,
        grid=(spans,),
        in_specs=[strip(INNER)] * 2
        + [strip(INNER)]
        + [strip(STATE, CONVW // STATE - 1)] * 2
        + [strip(HEADS)] * 2
        + [whole(length, INNER)] * 2
        + [whole(STATE, INNER)] * 2
        + [whole(spans, INNER)] * 2
        + [whole(1, INNER), whole(INNER, model), whole(model, model)],
        out_specs=strip(model),
        out_shape=like((length, model), BF16),
        scratch_shapes=[pltpu.VMEM((length, INNER), BF16)] * 2
        + [pltpu.VMEM((SPAN, INNER), F32)] * 2
        + [pltpu.VMEM((SPAN, INNER), BF16)],
        compiler_params=BIG,
        cost_estimate=cost(8e9, 20e6, 2e6),
        name="finish",
    )(
        y_f, y_b, projected, act_f, act_b, cum_f, cum_b, states_f, states_b, in_f, in_b,
        growth_f, growth_b, norm_gain[None], last_weight, turn,
    )

    first, second = out[:half], out[half:]
    mine = jnp.where(odd, second, first)
    back = lax.ppermute(jnp.where(odd, first, second), "seq", swap)
    return jnp.concatenate([jnp.where(odd, back, mine), jnp.where(odd, mine, back)], 1)[None]


def solution(mesh):
    placed = (
        P("batch", "seq", None), P("batch", None), P(), P(), P(), P(), P(), P(), P(),
        P("batch", None),
    )
    return jax.shard_map(
        on_device, mesh=mesh, in_specs=placed, out_specs=P("batch", "seq", None), check_vma=False
    )
```

```python
import jax
import jax.numpy as jnp
from jax import lax
from jax.experimental import pallas as pl
from jax.experimental.pallas import tpu as pltpu
from jax.sharding import PartitionSpec as P

INNER = 2048
HEADS = 32
STATE = 128
SPAN = 128
HEADDIM = 64
PAIRS = INNER // 128
CONVW = INNER + 2 * STATE
EDGE = 16
PIECES = 4
MESH = pl.DeviceIdType.MESH
F32 = jnp.float32
BF16 = jnp.bfloat16
BIG = pltpu.CompilerParams(vmem_limit_bytes=48 * 1024 * 1024)


def cost(flops, moved, exps):
    return pl.CostEstimate(flops=int(flops), bytes_accessed=int(moved), transcendentals=int(exps))


def silu(x):
    return x / (1.0 + jnp.exp(-x))


def spread(cells, pair):
    rows = cells.shape[0]
    low = jnp.broadcast_to(cells[:, 2 * pair : 2 * pair + 1], (rows, 128))
    high = jnp.broadcast_to(cells[:, 2 * pair + 1 : 2 * pair + 2], (rows, 128))
    return jnp.where(lax.broadcasted_iota(jnp.int32, (rows, 128), 1) < HEADDIM, low, high)


def states_kernel(
    proj, weight, bias, scaled_f, scaled_b, growth_f, growth_b,
    act_f, act_b, states_f, states_b, total_f, total_b, pad,
):
    length = act_f.shape[0]
    spans = length // SPAN

    @pl.loop(0, CONVW // 128)
    def _(j):
        cols = pl.ds(pl.multiple_of(j * 128, 128), 128)
        pad[0:EDGE, :] = proj[length : length + EDGE, cols].astype(F32)
        pad[EDGE : EDGE + length, :] = proj[0:length, cols].astype(F32)
        pad[EDGE + length :, :] = proj[length + EDGE :, cols].astype(F32)
        taps = [weight[k : k + 1, cols] for k in range(4)]
        start = bias[:, cols]
        for k in range(spans):
            base = k * SPAN + EDGE - 3
            ahead = start
            behind = start
            for tap in range(4):
                ahead = ahead + taps[tap] * pad[base + tap : base + tap + SPAN, :]
                behind = behind + taps[tap] * pad[base + 6 - tap : base + 6 - tap + SPAN, :]
            act_f[k * SPAN : (k + 1) * SPAN, cols] = silu(ahead).astype(BF16)
            act_b[k * SPAN : (k + 1) * SPAN, cols] = silu(behind).astype(BF16)

    for act, scaled, growth, states, total, order in (
        (act_f, scaled_f, growth_f, states_f, total_f, range(spans)),
        (act_b, scaled_b, growth_b, states_b, total_b, range(spans - 1, -1, -1)),
    ):

        @pl.loop(0, spans)
        def _(k):
            rows = pl.ds(pl.multiple_of(k * SPAN, SPAN), SPAN)
            write = act[rows, INNER : INNER + STATE].astype(F32).T.astype(BF16)
            scale = scaled[rows, :]
            for group in range(PAIRS // 2):
                parts = []
                for pair in (2 * group, 2 * group + 1):
                    vals = act[rows, pair * 128 : (pair + 1) * 128].astype(F32)
                    parts.append((vals * spread(scale, pair)).astype(BF16))
                states[rows, group * 256 : (group + 1) * 256] = jnp.dot(
                    write, jnp.concatenate(parts, 1), preferred_element_type=F32
                )

        for pair in range(PAIRS):
            cols = slice(pair * 128, (pair + 1) * 128)
            running = None
            for k in order:
                fresh = states[k * SPAN : (k + 1) * SPAN, cols]
                running = fresh if running is None else growth[k : k + 1, cols] * running + fresh
            total[:, cols] = running


def within_kernel(act_f, act_b, cum_f, cum_b, row_f, row_b, row_dt, skip, y_f, y_b):
    down = lax.broadcasted_iota(jnp.int32, (SPAN, SPAN), 0)
    across = lax.broadcasted_iota(jnp.int32, (SPAN, SPAN), 1)
    low_lanes = across < HEADDIM
    for act, cum, row, out, causal in (
        (act_f, cum_f, row_f, y_f, down >= across),
        (act_b, cum_b, row_b, y_b, down <= across),
    ):
        write = act[:, INNER : INNER + STATE]
        read = act[:, INNER + STATE :]
        scores = lax.dot_general(
            read, write, (((1,), (1,)), ((), ())), preferred_element_type=F32
        )
        column = cum[...]
        for pair in range(PAIRS):
            mixes = []
            for head in (2 * pair, 2 * pair + 1):
                gap = column[:, head : head + 1] - row[head : head + 1, :]
                decay = jnp.exp(jnp.where(causal, gap, -jnp.inf))
                mixes.append((scores * decay * row_dt[head : head + 1, :]).astype(BF16))
            cols = slice(pair * 128, (pair + 1) * 128)
            vals = act[:, cols]
            wide = vals.astype(F32)
            apart = jnp.concatenate(
                [
                    jnp.where(low_lanes, wide, 0.0).astype(BF16),
                    jnp.where(low_lanes, 0.0, wide).astype(BF16),
                ],
                0,
            )
            inner = jnp.dot(jnp.concatenate(mixes, 1), apart, preferred_element_type=F32)
            out[:, cols] = inner + skip[:, cols] * wide


def finish_kernel(
    y_f, y_b, gate, read_f, read_b, cum_f, cum_b, states_f, states_b, in_f, in_b,
    growth_f, growth_b, gain, weight, turn, out, entry_f, entry_b, gated_f, gated_b, comb,
):
    step = pl.program_id(0)
    spans = entry_f.shape[0] // SPAN

    @pl.when(step == 0)
    def _():
        for states, start, growth, entry, order in (
            (states_f, in_f, growth_f, entry_f, range(spans)),
            (states_b, in_b, growth_b, entry_b, range(spans - 1, -1, -1)),
        ):
            for pair in range(PAIRS):
                cols = slice(pair * 128, (pair + 1) * 128)
                running = start[:, cols].astype(F32)
                for k in order:
                    rows = slice(k * SPAN, (k + 1) * SPAN)
                    entry[rows, cols] = running.astype(BF16)
                    running = growth[k : k + 1, cols] * running + states[rows, cols]

    rows = pl.ds(pl.multiple_of(step * SPAN, SPAN), SPAN)
    scales = []
    grown_f, grown_b = jnp.exp(cum_f[...]), jnp.exp(cum_b[...])
    square_f = jnp.zeros((SPAN, 128), F32)
    square_b = jnp.zeros((SPAN, 128), F32)
    for group in range(PAIRS // 2):
        wide = slice(group * 256, (group + 1) * 256)
        from_f = jnp.dot(read_f[...], entry_f[rows, wide], preferred_element_type=F32)
        from_b = jnp.dot(read_b[...], entry_b[rows, wide], preferred_element_type=F32)
        for half in range(2):
            pair = 2 * group + half
            cols = slice(pair * 128, (pair + 1) * 128)
            part = slice(half * 128, (half + 1) * 128)
            opened = silu(gate[:, cols].astype(F32))
            v_f = (y_f[:, cols] + from_f[:, part] * spread(grown_f, pair)) * opened
            v_b = (y_b[:, cols] + from_b[:, part] * spread(grown_b, pair)) * opened
            gated_f[:, cols] = v_f
            gated_b[:, cols] = v_b
            square_f += v_f * v_f
            square_b += v_b * v_b
    scale_f = lax.rsqrt(jnp.sum(square_f, 1, keepdims=True) / INNER + 1e-5)
    scale_b = lax.rsqrt(jnp.sum(square_b, 1, keepdims=True) / INNER + 1e-5)
    for pair in range(PAIRS):
        cols = slice(pair * 128, (pair + 1) * 128)
        both = gated_f[:, cols] * scale_f + gated_b[:, cols] * scale_b
        comb[:, cols] = (both * gain[:, cols]).astype(BF16)
    stream = jnp.dot(comb[...], weight[...], preferred_element_type=F32).astype(BF16)
    out[...] = jnp.dot(stream, turn[...], preferred_element_type=F32).astype(BF16)


def chain_kernel(total_f, total_b, decay_f, decay_b, in_f, in_b, out_f, out_b, land_f, land_b, fsem, bsem):
    place, part = lax.axis_index("seq"), lax.axis_index("batch")
    count = lax.axis_size("seq")
    lower_there, upper_there = place >= 2, place + 2 < count
    barrier = pltpu.get_barrier_semaphore()
    for there, seat in ((lower_there, place - 2), (upper_there, place + 2)):

        @pl.when(there)
        def _(seat=seat):
            pl.semaphore_signal(barrier, inc=1, device_id=(seat, part), device_id_type=MESH)

    pl.semaphore_wait(barrier, lower_there.astype(jnp.int32) + upper_there.astype(jnp.int32))

    width = total_f.shape[1] // PIECES
    ways = (
        (total_f, decay_f, in_f, out_f, land_f, fsem, lower_there, upper_there, place + 2),
        (total_b, decay_b, in_b, out_b, land_b, bsem, upper_there, lower_there, place - 2),
    )

    def hop(way, piece):
        _, _, _, out, land, sems, _, _, seat = way
        return pltpu.make_async_remote_copy(
            src_ref=out.at[piece], dst_ref=land.at[piece], send_sem=sems.at[0, piece],
            recv_sem=sems.at[1, piece], device_id=(seat, part), device_id_type=MESH,
        )

    def begin(way):
        total, _, entry, out, _, _, source, target, _ = way

        @pl.when(jnp.logical_not(source))
        def _():
            for piece in range(PIECES):
                cols = slice(piece * width, (piece + 1) * width)
                out[piece] = total[:, cols].astype(BF16)
                hop(way, piece).start()
                entry[:, cols] = jnp.zeros((STATE, width), BF16)

    def relay(way, piece):
        total, decay, entry, out, land, _, source, target, _ = way
        cols = slice(piece * width, (piece + 1) * width)

        @pl.when(source)
        def _():
            hop(way, piece).wait_recv()

            @pl.when(target)
            def _():
                passed = decay[:, cols] * land[piece].astype(F32)
                out[piece] = (total[:, cols] + passed).astype(BF16)
                hop(way, piece).start()

            entry[:, cols] = land[piece]

    for way in ways:
        begin(way)

    nearer = place < count // 2
    for near, order in ((nearer, ways), (jnp.logical_not(nearer), ways[::-1])):

        @pl.when(near)
        def _(order=order):
            for piece in range(PIECES):
                for way in order:
                    relay(way, piece)

    for piece in range(PIECES):
        for way in ways:

            @pl.when(way[7])
            def _():
                hop(way, piece).wait_send()


def whole(*shape):
    return pl.BlockSpec(shape, lambda *_: (0,) * len(shape))


def on_device(
    hidden, in_weight, dt_weight, conv_weight, conv_bias, dt_bias, a_log, d_skip, norm_gain,
    out_weight,
):
    model = hidden.shape[2] // 2
    half = hidden.shape[1]
    length = 2 * half
    spans = length // SPAN
    count = lax.axis_size("seq")
    odd = lax.axis_index("seq") % 2 == 1
    swap = [(i, i ^ 1) for i in range(count)]

    like = jax.ShapeDtypeStruct
    dma = pltpu.SemaphoreType.DMA
    up = [(i, i + 2) for i in range(count - 2)]
    down = [(i + 2, i) for i in range(count - 2)]
    weight = lax.all_gather(in_weight[:, INNER:], "batch", axis=0, tiled=True)

    ahead_half, reverse_half = hidden[0, :, :model], hidden[0, :, model:]
    kept = jnp.where(odd, reverse_half, ahead_half)
    got = lax.ppermute(jnp.where(odd, ahead_half, reverse_half), "seq", swap)
    early, late = jnp.where(odd, got, kept), jnp.where(odd, kept, got)
    before = lax.ppermute(late[-EDGE:], "seq", up)
    after = lax.ppermute(early[:EDGE], "seq", down)
    rows = jnp.concatenate([early, late, before, after], 0)
    gate_shard, rows = lax.optimization_barrier((in_weight[:, :INNER], rows))
    gate_weight = lax.all_gather(gate_shard, "batch", axis=0, tiled=True)

    a = lax.broadcasted_iota(jnp.int32, (model, model), 0)
    b = lax.broadcasted_iota(jnp.int32, (model, model), 1)
    turn = jnp.where(odd, a + b == model - 1, a == b).astype(BF16)
    stream = jnp.dot(rows, turn, preferred_element_type=F32).astype(BF16)

    step = jax.nn.softplus(
        jnp.dot(stream[:length], dt_weight, preferred_element_type=F32) + dt_bias[None]
    )
    rates = (step * -jnp.exp(a_log)[None]).reshape(spans, SPAN, HEADS)
    place = jnp.arange(SPAN)
    lower = (place[:, None] >= place[None]).astype(F32)
    high = lax.Precision.HIGHEST
    cum_f = jnp.einsum("ts,ksh->kth", lower, rates, precision=high)
    cum_b = jnp.einsum("ts,ksh->kth", lower.T, rates, precision=high)
    end_f, end_b = cum_f[:, -1], cum_b[:, 0]
    step_spans = step.reshape(spans, SPAN, HEADS)
    scaled_f = (jnp.exp(end_f[:, None] - cum_f) * step_spans).reshape(length, HEADS)
    scaled_b = (jnp.exp(end_b[:, None] - cum_b) * step_spans).reshape(length, HEADS)
    growth_f = jnp.repeat(jnp.exp(end_f), HEADDIM, 1)
    growth_b = jnp.repeat(jnp.exp(end_b), HEADDIM, 1)
    cum_f, cum_b = cum_f.reshape(length, HEADS), cum_b.reshape(length, HEADS)
    row_f, row_b, row_dt = cum_f.T, cum_b.T, step.T

    projected = jnp.dot(stream, weight, preferred_element_type=F32).astype(BF16)
    act_f, act_b, states_f, states_b, total_f, total_b = pl.pallas_call(
        states_kernel,
        out_shape=[like((length, CONVW), BF16)] * 2
        + [like((length, INNER), F32)] * 2
        + [like((STATE, INNER), F32)] * 2,
        scratch_shapes=[pltpu.VMEM((length + 2 * EDGE, 128), F32)],
        compiler_params=BIG,
        cost_estimate=cost(8e9, 20e6, 3e6),
        name="states",
    )(
        projected, conv_weight, conv_bias[None], scaled_f, scaled_b, growth_f, growth_b,
    )

    out_weight, total_f = lax.optimization_barrier((out_weight, total_f))
    last_weight = lax.all_gather(out_weight, "batch", axis=0, tiled=True)
    in_f, in_b = pl.pallas_call(
        chain_kernel,
        out_shape=[like((STATE, INNER), BF16)] * 2,
        scratch_shapes=[pltpu.VMEM((PIECES, STATE, INNER // PIECES), BF16)] * 4
        + [dma((2, PIECES))] * 2,
        compiler_params=pltpu.CompilerParams(
            collective_id=1, has_side_effects=True, vmem_limit_bytes=32 * 1024 * 1024
        ),
        cost_estimate=cost(2e6, 8e6, 0),
        name="chain",
    )(total_f, total_b, jnp.prod(growth_f, 0)[None], jnp.prod(growth_b, 0)[None])

    def strip(width, at=0):
        return pl.BlockSpec((SPAN, width), lambda k: (k, at))

    def slab():
        return pl.BlockSpec((HEADS, SPAN), lambda k: (0, k))

    gate_weight, in_f = lax.optimization_barrier((gate_weight, in_f))
    gate = jnp.dot(stream[:length], gate_weight, preferred_element_type=F32).astype(BF16)

    y_f, y_b = pl.pallas_call(
        within_kernel,
        grid=(spans,),
        in_specs=[strip(CONVW)] * 2 + [strip(HEADS)] * 2 + [slab()] * 3 + [whole(1, INNER)],
        out_specs=[strip(INNER)] * 2,
        out_shape=[like((length, INNER), F32)] * 2,
        compiler_params=BIG,
        cost_estimate=cost(25e9, 15e6, 5e6),
        name="within",
    )(act_f, act_b, cum_f, cum_b, row_f, row_b, row_dt, jnp.repeat(d_skip, HEADDIM)[None])

    out = pl.pallas_call(
        finish_kernel,
        grid=(spans,),
        in_specs=[strip(INNER)] * 2
        + [strip(INNER)]
        + [strip(STATE, CONVW // STATE - 1)] * 2
        + [strip(HEADS)] * 2
        + [whole(length, INNER)] * 2
        + [whole(STATE, INNER)] * 2
        + [whole(spans, INNER)] * 2
        + [whole(1, INNER), whole(INNER, model), whole(model, model)],
        out_specs=strip(model),
        out_shape=like((length, model), BF16),
        scratch_shapes=[pltpu.VMEM((length, INNER), BF16)] * 2
        + [pltpu.VMEM((SPAN, INNER), F32)] * 2
        + [pltpu.VMEM((SPAN, INNER), BF16)],
        compiler_params=BIG,
        cost_estimate=cost(8e9, 20e6, 2e6),
        name="finish",
    )(
        y_f, y_b, gate, act_f, act_b, cum_f, cum_b, states_f, states_b, in_f, in_b,
        growth_f, growth_b, norm_gain[None], last_weight, turn,
    )

    first, second = out[:half], out[half:]
    mine = jnp.where(odd, second, first)
    back = lax.ppermute(jnp.where(odd, first, second), "seq", swap)
    return jnp.concatenate([jnp.where(odd, back, mine), jnp.where(odd, mine, back)], 1)[None]


def solution(mesh):
    placed = (
        P("batch", "seq", None), P("batch", None), P(), P(), P(), P(), P(), P(), P(),
        P("batch", None),
    )
    return jax.shard_map(
        on_device, mesh=mesh, in_specs=placed, out_specs=P("batch", "seq", None), check_vma=False
    )
```

```python
import jax
import jax.numpy as jnp
from jax import lax
from jax.experimental import pallas as pl
from jax.experimental.pallas import tpu as pltpu
from jax.sharding import PartitionSpec as P

INNER = 2048
HEADS = 32
STATE = 128
SPAN = 128
HEADDIM = 64
PAIRS = INNER // 128
CONVW = INNER + 2 * STATE
EDGE = 16
PIECES = 8
MESH = pl.DeviceIdType.MESH
F32 = jnp.float32
BF16 = jnp.bfloat16
BIG = pltpu.CompilerParams(vmem_limit_bytes=48 * 1024 * 1024)


def cost(flops, moved, exps):
    return pl.CostEstimate(flops=int(flops), bytes_accessed=int(moved), transcendentals=int(exps))


def silu(x):
    return x / (1.0 + jnp.exp(-x))


def spread(cells, pair):
    rows = cells.shape[0]
    low = jnp.broadcast_to(cells[:, 2 * pair : 2 * pair + 1], (rows, 128))
    high = jnp.broadcast_to(cells[:, 2 * pair + 1 : 2 * pair + 2], (rows, 128))
    return jnp.where(lax.broadcasted_iota(jnp.int32, (rows, 128), 1) < HEADDIM, low, high)


def states_kernel(
    proj, weight, bias, scaled_f, scaled_b, growth_f, growth_b,
    act_f, act_b, states_f, states_b, total_f, total_b, pad,
):
    length = act_f.shape[0]
    spans = length // SPAN

    @pl.loop(0, CONVW // 128)
    def _(j):
        cols = pl.ds(pl.multiple_of(j * 128, 128), 128)
        pad[0:EDGE, :] = proj[length : length + EDGE, cols].astype(F32)
        pad[EDGE : EDGE + length, :] = proj[0:length, cols].astype(F32)
        pad[EDGE + length :, :] = proj[length + EDGE :, cols].astype(F32)
        taps = [weight[k : k + 1, cols] for k in range(4)]
        start = bias[:, cols]
        for k in range(spans):
            base = k * SPAN + EDGE - 3
            ahead = start
            behind = start
            for tap in range(4):
                ahead = ahead + taps[tap] * pad[base + tap : base + tap + SPAN, :]
                behind = behind + taps[tap] * pad[base + 6 - tap : base + 6 - tap + SPAN, :]
            act_f[k * SPAN : (k + 1) * SPAN, cols] = silu(ahead).astype(BF16)
            act_b[k * SPAN : (k + 1) * SPAN, cols] = silu(behind).astype(BF16)

    for act, scaled, growth, states, total, order in (
        (act_f, scaled_f, growth_f, states_f, total_f, range(spans)),
        (act_b, scaled_b, growth_b, states_b, total_b, range(spans - 1, -1, -1)),
    ):

        @pl.loop(0, spans)
        def _(k):
            rows = pl.ds(pl.multiple_of(k * SPAN, SPAN), SPAN)
            write = act[rows, INNER : INNER + STATE].astype(F32).T.astype(BF16)
            scale = scaled[rows, :]
            for group in range(PAIRS // 2):
                parts = []
                for pair in (2 * group, 2 * group + 1):
                    vals = act[rows, pair * 128 : (pair + 1) * 128].astype(F32)
                    parts.append((vals * spread(scale, pair)).astype(BF16))
                states[rows, group * 256 : (group + 1) * 256] = jnp.dot(
                    write, jnp.concatenate(parts, 1), preferred_element_type=F32
                )

        for pair in range(PAIRS):
            cols = slice(pair * 128, (pair + 1) * 128)
            running = None
            for k in order:
                fresh = states[k * SPAN : (k + 1) * SPAN, cols]
                running = fresh if running is None else growth[k : k + 1, cols] * running + fresh
            total[:, cols] = running


def within_kernel(act_f, act_b, cum_f, cum_b, row_f, row_b, row_dt, skip, y_f, y_b):
    down = lax.broadcasted_iota(jnp.int32, (SPAN, SPAN), 0)
    across = lax.broadcasted_iota(jnp.int32, (SPAN, SPAN), 1)
    low_lanes = across < HEADDIM
    for act, cum, row, out, causal in (
        (act_f, cum_f, row_f, y_f, down >= across),
        (act_b, cum_b, row_b, y_b, down <= across),
    ):
        write = act[:, INNER : INNER + STATE]
        read = act[:, INNER + STATE :]
        scores = lax.dot_general(
            read, write, (((1,), (1,)), ((), ())), preferred_element_type=F32
        )
        column = cum[...]
        for pair in range(PAIRS):
            mixes = []
            for head in (2 * pair, 2 * pair + 1):
                gap = column[:, head : head + 1] - row[head : head + 1, :]
                decay = jnp.exp(jnp.where(causal, gap, -jnp.inf))
                mixes.append((scores * decay * row_dt[head : head + 1, :]).astype(BF16))
            cols = slice(pair * 128, (pair + 1) * 128)
            vals = act[:, cols]
            wide = vals.astype(F32)
            apart = jnp.concatenate(
                [
                    jnp.where(low_lanes, wide, 0.0).astype(BF16),
                    jnp.where(low_lanes, 0.0, wide).astype(BF16),
                ],
                0,
            )
            inner = jnp.dot(jnp.concatenate(mixes, 1), apart, preferred_element_type=F32)
            out[:, cols] = inner + skip[:, cols] * wide


def finish_kernel(
    y_f, y_b, gate, read_f, read_b, cum_f, cum_b, states_f, states_b, in_f, in_b,
    growth_f, growth_b, gain, weight, turn, out, entry_f, entry_b, gated_f, gated_b, comb,
):
    step = pl.program_id(0)
    spans = entry_f.shape[0] // SPAN

    @pl.when(step == 0)
    def _():
        for states, start, growth, entry, order in (
            (states_f, in_f, growth_f, entry_f, range(spans)),
            (states_b, in_b, growth_b, entry_b, range(spans - 1, -1, -1)),
        ):
            for pair in range(PAIRS):
                cols = slice(pair * 128, (pair + 1) * 128)
                running = start[:, cols].astype(F32)
                for k in order:
                    rows = slice(k * SPAN, (k + 1) * SPAN)
                    entry[rows, cols] = running.astype(BF16)
                    running = growth[k : k + 1, cols] * running + states[rows, cols]

    rows = pl.ds(pl.multiple_of(step * SPAN, SPAN), SPAN)
    scales = []
    grown_f, grown_b = jnp.exp(cum_f[...]), jnp.exp(cum_b[...])
    square_f = jnp.zeros((SPAN, 128), F32)
    square_b = jnp.zeros((SPAN, 128), F32)
    for group in range(PAIRS // 2):
        wide = slice(group * 256, (group + 1) * 256)
        from_f = jnp.dot(read_f[...], entry_f[rows, wide], preferred_element_type=F32)
        from_b = jnp.dot(read_b[...], entry_b[rows, wide], preferred_element_type=F32)
        for half in range(2):
            pair = 2 * group + half
            cols = slice(pair * 128, (pair + 1) * 128)
            part = slice(half * 128, (half + 1) * 128)
            opened = silu(gate[:, cols].astype(F32))
            v_f = (y_f[:, cols] + from_f[:, part] * spread(grown_f, pair)) * opened
            v_b = (y_b[:, cols] + from_b[:, part] * spread(grown_b, pair)) * opened
            gated_f[:, cols] = v_f
            gated_b[:, cols] = v_b
            square_f += v_f * v_f
            square_b += v_b * v_b
    scale_f = lax.rsqrt(jnp.sum(square_f, 1, keepdims=True) / INNER + 1e-5)
    scale_b = lax.rsqrt(jnp.sum(square_b, 1, keepdims=True) / INNER + 1e-5)
    for pair in range(PAIRS):
        cols = slice(pair * 128, (pair + 1) * 128)
        both = gated_f[:, cols] * scale_f + gated_b[:, cols] * scale_b
        comb[:, cols] = (both * gain[:, cols]).astype(BF16)
    stream = jnp.dot(comb[...], weight[...], preferred_element_type=F32).astype(BF16)
    out[...] = jnp.dot(stream, turn[...], preferred_element_type=F32).astype(BF16)


def chain_kernel(total_f, total_b, decay_f, decay_b, in_f, in_b, out_f, out_b, land_f, land_b, fsem, bsem):
    place, part = lax.axis_index("seq"), lax.axis_index("batch")
    count = lax.axis_size("seq")
    lower_there, upper_there = place >= 2, place + 2 < count
    barrier = pltpu.get_barrier_semaphore()
    for there, seat in ((lower_there, place - 2), (upper_there, place + 2)):

        @pl.when(there)
        def _(seat=seat):
            pl.semaphore_signal(barrier, inc=1, device_id=(seat, part), device_id_type=MESH)

    pl.semaphore_wait(barrier, lower_there.astype(jnp.int32) + upper_there.astype(jnp.int32))

    width = total_f.shape[1] // PIECES
    ways = (
        (total_f, decay_f, in_f, out_f, land_f, fsem, lower_there, upper_there, place + 2),
        (total_b, decay_b, in_b, out_b, land_b, bsem, upper_there, lower_there, place - 2),
    )

    def hop(way, piece):
        _, _, _, out, land, sems, _, _, seat = way
        return pltpu.make_async_remote_copy(
            src_ref=out.at[piece], dst_ref=land.at[piece], send_sem=sems.at[0, piece],
            recv_sem=sems.at[1, piece], device_id=(seat, part), device_id_type=MESH,
        )

    def begin(way):
        total, _, entry, out, _, _, source, target, _ = way

        @pl.when(jnp.logical_not(source))
        def _():
            for piece in range(PIECES):
                cols = slice(piece * width, (piece + 1) * width)
                out[piece] = total[:, cols].astype(BF16)
                hop(way, piece).start()
                entry[:, cols] = jnp.zeros((STATE, width), BF16)

    def relay(way, piece):
        total, decay, entry, out, land, _, source, target, _ = way
        cols = slice(piece * width, (piece + 1) * width)

        @pl.when(source)
        def _():
            hop(way, piece).wait_recv()

            @pl.when(target)
            def _():
                passed = decay[:, cols] * land[piece].astype(F32)
                out[piece] = (total[:, cols] + passed).astype(BF16)
                hop(way, piece).start()

            entry[:, cols] = land[piece]

    for way in ways:
        begin(way)

    nearer = place < count // 2
    for near, order in ((nearer, ways), (jnp.logical_not(nearer), ways[::-1])):

        @pl.when(near)
        def _(order=order):
            for piece in range(PIECES):
                for way in order:
                    relay(way, piece)

    for piece in range(PIECES):
        for way in ways:

            @pl.when(way[7])
            def _():
                hop(way, piece).wait_send()


def whole(*shape):
    return pl.BlockSpec(shape, lambda *_: (0,) * len(shape))


def on_device(
    hidden, in_weight, dt_weight, conv_weight, conv_bias, dt_bias, a_log, d_skip, norm_gain,
    out_weight,
):
    model = hidden.shape[2] // 2
    half = hidden.shape[1]
    length = 2 * half
    spans = length // SPAN
    count = lax.axis_size("seq")
    odd = lax.axis_index("seq") % 2 == 1
    swap = [(i, i ^ 1) for i in range(count)]

    like = jax.ShapeDtypeStruct
    dma = pltpu.SemaphoreType.DMA
    up = [(i, i + 2) for i in range(count - 2)]
    down = [(i + 2, i) for i in range(count - 2)]
    weight = lax.all_gather(in_weight[:, INNER:], "batch", axis=0, tiled=True)

    ahead_half, reverse_half = hidden[0, :, :model], hidden[0, :, model:]
    kept = jnp.where(odd, reverse_half, ahead_half)
    got = lax.ppermute(jnp.where(odd, ahead_half, reverse_half), "seq", swap)
    early, late = jnp.where(odd, got, kept), jnp.where(odd, kept, got)
    before = lax.ppermute(late[-EDGE:], "seq", up)
    after = lax.ppermute(early[:EDGE], "seq", down)
    rows = jnp.concatenate([early, late, before, after], 0)
    gate_shard, rows = lax.optimization_barrier((in_weight[:, :INNER], rows))
    gate_weight = lax.all_gather(gate_shard, "batch", axis=0, tiled=True)

    a = lax.broadcasted_iota(jnp.int32, (model, model), 0)
    b = lax.broadcasted_iota(jnp.int32, (model, model), 1)
    turn = jnp.where(odd, a + b == model - 1, a == b).astype(BF16)
    stream = jnp.dot(rows, turn, preferred_element_type=F32).astype(BF16)

    step = jax.nn.softplus(
        jnp.dot(stream[:length], dt_weight, preferred_element_type=F32) + dt_bias[None]
    )
    rates = (step * -jnp.exp(a_log)[None]).reshape(spans, SPAN, HEADS)
    place = jnp.arange(SPAN)
    lower = (place[:, None] >= place[None]).astype(F32)
    high = lax.Precision.HIGHEST
    cum_f = jnp.einsum("ts,ksh->kth", lower, rates, precision=high)
    cum_b = jnp.einsum("ts,ksh->kth", lower.T, rates, precision=high)
    end_f, end_b = cum_f[:, -1], cum_b[:, 0]
    step_spans = step.reshape(spans, SPAN, HEADS)
    scaled_f = (jnp.exp(end_f[:, None] - cum_f) * step_spans).reshape(length, HEADS)
    scaled_b = (jnp.exp(end_b[:, None] - cum_b) * step_spans).reshape(length, HEADS)
    growth_f = jnp.repeat(jnp.exp(end_f), HEADDIM, 1)
    growth_b = jnp.repeat(jnp.exp(end_b), HEADDIM, 1)
    cum_f, cum_b = cum_f.reshape(length, HEADS), cum_b.reshape(length, HEADS)
    row_f, row_b, row_dt = cum_f.T, cum_b.T, step.T

    projected = jnp.dot(stream, weight, preferred_element_type=F32).astype(BF16)
    act_f, act_b, states_f, states_b, total_f, total_b = pl.pallas_call(
        states_kernel,
        out_shape=[like((length, CONVW), BF16)] * 2
        + [like((length, INNER), F32)] * 2
        + [like((STATE, INNER), F32)] * 2,
        scratch_shapes=[pltpu.VMEM((length + 2 * EDGE, 128), F32)],
        compiler_params=BIG,
        cost_estimate=cost(8e9, 20e6, 3e6),
        name="states",
    )(
        projected, conv_weight, conv_bias[None], scaled_f, scaled_b, growth_f, growth_b,
    )

    out_weight, total_f = lax.optimization_barrier((out_weight, total_f))
    last_weight = lax.all_gather(out_weight, "batch", axis=0, tiled=True)
    in_f, in_b = pl.pallas_call(
        chain_kernel,
        out_shape=[like((STATE, INNER), BF16)] * 2,
        scratch_shapes=[pltpu.VMEM((PIECES, STATE, INNER // PIECES), BF16)] * 4
        + [dma((2, PIECES))] * 2,
        compiler_params=pltpu.CompilerParams(
            collective_id=1, has_side_effects=True, vmem_limit_bytes=32 * 1024 * 1024
        ),
        cost_estimate=cost(2e6, 8e6, 0),
        name="chain",
    )(total_f, total_b, jnp.prod(growth_f, 0)[None], jnp.prod(growth_b, 0)[None])

    def strip(width, at=0):
        return pl.BlockSpec((SPAN, width), lambda k: (k, at))

    def slab():
        return pl.BlockSpec((HEADS, SPAN), lambda k: (0, k))

    gate_weight, in_f = lax.optimization_barrier((gate_weight, in_f))
    gate = jnp.dot(stream[:length], gate_weight, preferred_element_type=F32).astype(BF16)

    y_f, y_b = pl.pallas_call(
        within_kernel,
        grid=(spans,),
        in_specs=[strip(CONVW)] * 2 + [strip(HEADS)] * 2 + [slab()] * 3 + [whole(1, INNER)],
        out_specs=[strip(INNER)] * 2,
        out_shape=[like((length, INNER), F32)] * 2,
        compiler_params=BIG,
        cost_estimate=cost(25e9, 15e6, 5e6),
        name="within",
    )(act_f, act_b, cum_f, cum_b, row_f, row_b, row_dt, jnp.repeat(d_skip, HEADDIM)[None])

    out = pl.pallas_call(
        finish_kernel,
        grid=(spans,),
        in_specs=[strip(INNER)] * 2
        + [strip(INNER)]
        + [strip(STATE, CONVW // STATE - 1)] * 2
        + [strip(HEADS)] * 2
        + [whole(length, INNER)] * 2
        + [whole(STATE, INNER)] * 2
        + [whole(spans, INNER)] * 2
        + [whole(1, INNER), whole(INNER, model), whole(model, model)],
        out_specs=strip(model),
        out_shape=like((length, model), BF16),
        scratch_shapes=[pltpu.VMEM((length, INNER), BF16)] * 2
        + [pltpu.VMEM((SPAN, INNER), F32)] * 2
        + [pltpu.VMEM((SPAN, INNER), BF16)],
        compiler_params=BIG,
        cost_estimate=cost(8e9, 20e6, 2e6),
        name="finish",
    )(
        y_f, y_b, gate, act_f, act_b, cum_f, cum_b, states_f, states_b, in_f, in_b,
        growth_f, growth_b, norm_gain[None], last_weight, turn,
    )

    first, second = out[:half], out[half:]
    mine = jnp.where(odd, second, first)
    back = lax.ppermute(jnp.where(odd, first, second), "seq", swap)
    return jnp.concatenate([jnp.where(odd, back, mine), jnp.where(odd, mine, back)], 1)[None]


def solution(mesh):
    placed = (
        P("batch", "seq", None), P("batch", None), P(), P(), P(), P(), P(), P(), P(),
        P("batch", None),
    )
    return jax.shard_map(
        on_device, mesh=mesh, in_specs=placed, out_specs=P("batch", "seq", None), check_vma=False
    )
```
